256 devices in a mesh: wide: 64 (over x, z, y_lo), loop: 4 (over y_hi, core).
Axes of the slice: x: 4, y: 4 (y_hi: 2, y_lo: 2; y = y_hi * 2 + y_lo), z: 8, core: 2. Of those that a mesh axis runs over, the one named last changes fastest.
Arguments:
- diag_block: float32 [512, 512], P('wide')
- panel: float32 [98304, 512], P('wide'), may hold values from -12 to 12
- trailing: float32 [98304, 4096], P('wide', 'loop'), may hold values from -6 to 6
- fill_mask: int32 [768, 32], P('wide', 'loop'), may hold values 0 or 1
- column_tiles: int32 [32], P('loop'), may hold values from 0 to 767
Outputs:
- updated: float32 [98304, 4096], P('wide', 'loop')
The draws below stay inside these ranges and needn't reach their ends.
All inputs are finite; a program needn't handle non-finite values. No bound on the sum of `fill_mask` on one device may be relied on, other than what follows from the above.
Results may differ from the reference program's by a relative error of at most 0.00005.
Values sent between devices are 32-bit elements; how exact they have to be, the bound alone decides.
A program may use at most 128 MiB of HBM per device.

```python
import jax
import jax.numpy as jnp
from jax import lax

PANEL = 512
TILE = 128
ROW_TILES = 768
COL_TILES = 32
ROWS = 98304
COLS = 4096


def draw_diag_block(key, part):
    key_off = jax.random.fold_in(key, 11)
    key_diag = jax.random.fold_in(key, 12)
    off_diag = jax.random.uniform(key_off, (PANEL, PANEL), jnp.float32, -1.0, 1.0)
    off_diag = (off_diag + off_diag.T) * (25.0 / PANEL)
    main_diag = jax.random.uniform(key_diag, (PANEL,), jnp.float32, 60.0, 120.0)
    marker = jnp.arange(PANEL)[:, None] == jnp.arange(PANEL)[None, :]
    return jnp.where(marker, main_diag[:, None], off_diag).astype(jnp.float32)


def with_ends(result, rng, smallest, top_value):
    longest = result.shape.index(max(result.shape))
    spots = []
    for shift in (0, 1):
        where = [jax.random.randint(jax.random.fold_in(rng, axis), (), 0, length) for axis, length in enumerate(result.shape)]
        where[longest] = (where[longest] + shift) % result.shape[longest]
        spots.append(tuple(where))
    return result.at[spots[0]].set(smallest).at[spots[1]].set(top_value)


def block_levels(stream_key, dims, shards, smallest, top_value):
    loudness = 1.0
    for axis_at, shards_of in shards:
        heights = jax.random.uniform(jax.random.fold_in(jax.random.fold_in(stream_key, 6), axis_at), (shards_of,), jnp.float32, smallest / len(shards), top_value / len(shards))
        loudness = loudness * jnp.repeat(jnp.exp(heights), dims[axis_at] // shards_of).reshape((-1,) + (1,) * (len(dims) - 1 - axis_at))
    return loudness


def centred(rng, extent, scale, limit, cuts=(), kind=jnp.bfloat16):
    values = scale * jax.random.normal(rng, extent, jnp.float32)
    if cuts:
        values = values * block_levels(rng, extent, cuts, -0.22, 0.18)
    return jnp.clip(values, -limit, limit).astype(kind)


def setup_inputs(seed: int = 0) -> dict:
    splits = jax.random.split(jax.random.key(seed), 6)
    return {
        "diag_block": draw_diag_block(jax.random.fold_in(splits[5], 71), 0),
        "panel": centred(splits[1], (ROWS, PANEL), 2.0, 12.0, ((0, 64),), jnp.float32),
        "trailing": centred(splits[2], (ROWS, COLS), 1.0, 6.0, ((0, 64), (1, 4)), jnp.float32),
        "fill_mask": with_ends((jax.random.randint(splits[3], (ROW_TILES, COL_TILES), 0, 2) < 1).astype(jnp.int32), jax.random.fold_in(splits[3], 1), 0, 1),
        "column_tiles": with_ends(jax.random.randint(splits[4], (COL_TILES,), 0, ROW_TILES), jax.random.fold_in(splits[4], 1), 0, ROW_TILES - 1).astype(jnp.int32),
    }


def reference(diag_block, panel, trailing, fill_mask, column_tiles):
    precise = lax.Precision.HIGHEST
    factor = jnp.linalg.cholesky(diag_block)
    lower_panel = jax.scipy.linalg.solve_triangular(factor, panel.T, lower=True).T
    picked = lower_panel.reshape(ROW_TILES, TILE, PANEL)[column_tiles.astype(jnp.int32)].reshape(COLS, PANEL)
    update = jnp.dot(lower_panel, picked.T, precision=precise)
    weights = jnp.repeat(jnp.repeat(fill_mask.astype(jnp.float32), TILE, axis=0), TILE, axis=1)
    return trailing - weights * update
```

```python
import functools
import math

import jax
import jax.numpy as jnp
from jax import lax
from jax.experimental import pallas as pl
from jax.experimental.pallas import tpu as pltpu
from jax.sharding import PartitionSpec as P

F32, BF16 = jnp.float32, jnp.bfloat16
HI = lax.Precision.HIGHEST
MESH = pl.DeviceIdType.MESH
SUB, WIDE, LANES = 8, 128, 128
NT = (((1,), (1,)), ((), ()))
NN = (((1,), (0,)), ((), ()))
DIMS = (4, 8, 2)
SHARES = (((0, 1, 2), 3), ((2, 0, 1), 3), ((1, 0, 2), 2))


def lane_bcast(x, lane):
    return jnp.broadcast_to(x[:, lane:lane + 1], (SUB, WIDE))

def sub_bcast(x, row):
    return jnp.broadcast_to(x[row:row + 1, :], (SUB, WIDE))

def factor_tile(rows):
    lane = lax.broadcasted_iota(jnp.int32, (SUB, WIDE), 1)
    sub = lax.broadcasted_iota(jnp.int32, (SUB, WIDE), 0)
    rows = list(rows)
    count = len(rows)
    scales = []
    for k in range(count):
        base = SUB * k
        here = (lane >= base) & (lane < base + SUB)
        own = rows[k]
        cols = [lane_bcast(own, base + p) for p in range(SUB)]
        own = jnp.where(here, jnp.where(lane - base == sub, 1.0, 0.0), own)
        invs, tops, edges = [], [], {}
        scale = jnp.ones((SUB, WIDE), F32)
        for p in range(SUB):
            inv = 1.0 / sub_bcast(cols[p], p)
            invs.append(inv)
            scale = jnp.where(sub == p, inv, scale)
            top = sub_bcast(own, p)
            tops.append(top)
            if p < SUB - 1:
                mult = jnp.where(sub > p, cols[p] * inv, 0.0)
                for q in range(p + 1, SUB):
                    edges[p, q] = sub_bcast(cols[q], p)
                    cols[q] = cols[q] - mult * edges[p, q]
                own = own - mult * top
        rows[k] = own
        scales.append(scale)
        for i in range(k + 1, count):
            below = [lane_bcast(rows[i], base + p) for p in range(SUB)]
            new = jnp.where(here, 0.0, rows[i])
            for p in range(SUB):
                mult = below[p] * invs[p]
                for q in range(p + 1, SUB):
                    below[q] = below[q] - mult * edges[p, q]
                new = new - mult * tops[p]
            rows[i] = new
    return rows, scales

def factor_inverse(a, w, n):
    tiles = n // WIDE
    lane = lax.broadcasted_iota(jnp.int32, (WIDE, WIDE), 1)
    sub = lax.broadcasted_iota(jnp.int32, (WIDE, WIDE), 0)
    w[...] = jnp.zeros_like(w)
    for j in range(tiles):
        lo, hi = j * WIDE, (j + 1) * WIDE
        rows = [a[lo + SUB * k: lo + SUB * (k + 1), lo:hi] for k in range(WIDE // SUB)]
        rows, scales = factor_tile(rows)
        linv = jnp.concatenate(rows, axis=0)
        linv = jnp.where(lane <= sub, linv, 0.0)
        inv = jnp.concatenate(scales, axis=0)
        root = jnp.sqrt(inv)
        w[lo:hi, lo:hi] = linv * root
        if j + 1 < tiles:
            right = jnp.dot(linv, a[lo:hi, hi:], precision=HI, preferred_element_type=F32)
            mult = lax.dot_general(a[hi:, lo:hi], linv, (((1,), (1,)), ((), ())), precision=HI, preferred_element_type=F32)
        if j:
            left = jnp.dot(linv, a[lo:hi, :lo], precision=HI, preferred_element_type=F32)
            w[lo:hi, :lo] = left * jnp.concatenate([root] * j, axis=1)
        if j + 1 < tiles:
            sc = jnp.concatenate([inv] * (tiles - 1 - j), axis=1)
            a[hi:, hi:] = a[hi:, hi:] - jnp.dot(mult, right * sc, precision=HI, preferred_element_type=F32)
            a[hi:, lo:hi] = -jnp.dot(mult, linv * inv, precision=HI, preferred_element_type=F32)
            if j:
                a[hi:, :lo] = a[hi:, :lo] - jnp.dot(mult, left * jnp.concatenate([inv] * j, axis=1), precision=HI, preferred_element_type=F32)


class Net:
    def __init__(self, dims, send, recv):
        self.dims = dims
        me = lax.axis_index("wide")
        nx, nz, ny = dims
        self.me = (me // (nz * ny), (me // ny) % nz, me % ny)
        self.send, self.recv, self.used = send, recv, 0

    def peer(self, axis, step):
        c = list(self.me)
        c[axis] = lax.rem(c[axis] + step, self.dims[axis])
        return c[axis], (c[0] * self.dims[1] + c[1]) * self.dims[2] + c[2]

    def copy(self, src, dst, wide):
        i = self.used
        self.used += 1
        c = pltpu.make_async_remote_copy(src_ref=src, dst_ref=dst, send_sem=self.send.at[i], recv_sem=self.recv.at[i],
                                         device_id={"wide": wide}, device_id_type=MESH)
        c.start()
        return c

def greet(net):
    barrier = pltpu.get_barrier_semaphore()
    total = 0
    for axis in range(3):
        for step in range(1, net.dims[axis]):
            pl.semaphore_signal(barrier, inc=1, device_id={"wide": net.peer(axis, step)[1]}, device_id_type=MESH)
            total += 1
    pl.semaphore_wait(barrier, total)

class Fraction:
    def __init__(self, net, q, out, start, unit, order, bufs):
        self.net, self.q, self.out, self.start, self.order = net, q, out, start, order
        self.sizes = [net.dims[a] for a in order]
        self.coords = [net.me[a] for a in order]
        n1, n2, n3 = self.sizes
        self.blocks = [unit * n2 * n3, unit * n3, unit]
        self.bufs = bufs
        self.pending = []

    def scatter_start(self, level):
        size = self.blocks[level]
        src, base = (self.q, self.start) if level == 0 else (self.bufs[level - 1][1], 0)
        self.pending = []
        for step in range(1, self.sizes[level]):
            at, wide = self.net.peer(self.order[level], step)
            rows = pl.ds(pl.multiple_of(base + at * size, 8), size)
            self.pending.append(self.net.copy(src.at[rows], self.bufs[level][0].at[step - 1], wide))

    def scatter_finish(self, level):
        size = self.blocks[level]
        src, base = (self.q, self.start) if level == 0 else (self.bufs[level - 1][1], 0)
        for c in self.pending:
            c.wait()
        got, total = self.bufs[level]
        acc = src[pl.ds(pl.multiple_of(base + self.coords[level] * size, 8), size), :]
        for step in range(1, self.sizes[level]):
            acc = acc + got[step - 1]
        if level < 2:
            total[...] = acc
        else:
            self.out[pl.ds(self.offset(2), size), :] = acc

    def offset(self, level):
        at = self.start
        for l in range(level + 1):
            at = at + self.coords[l] * self.blocks[l]
        return pl.multiple_of(at, 8)

    def gather_start(self, level):
        rows = pl.ds(self.offset(level), self.blocks[level])
        self.pending = []
        for step in range(1, self.sizes[level]):
            _, wide = self.net.peer(self.order[level], step)
            self.pending.append(self.net.copy(self.out.at[rows], self.out.at[rows], wide))

    def gather_finish(self):
        for c in self.pending:
            c.wait()

class Diag:
    def __init__(self, net, g):
        self.net, self.g, self.pending = net, g, []

    def view(self, axis):
        x, z, y = self.net.me
        return self.g.at[x, z, y] if axis == 2 else self.g.at[x, z] if axis == 1 else self.g.at[x]

    def start(self, axis):
        self.pending = []
        for step in range(1, self.net.dims[axis]):
            _, wide = self.net.peer(axis, step)
            self.pending.append(self.net.copy(self.view(axis), self.view(axis), wide))

    def finish(self):
        for c in self.pending:
            c.wait()

def plan(dims, total, shares):
    devices = math.prod(dims)
    units = total // (8 * devices)
    out, start = [], 0
    for order, share in shares:
        unit = 8 * share
        out.append((start, unit, order))
        start += unit * devices
    assert start == total
    return out

def scratch_for(dims, parts):
    shapes = []
    for start, unit, order in parts:
        n1, n2, n3 = [dims[a] for a in order]
        shapes += [pltpu.VMEM((n1 - 1, unit * n2 * n3, LANES), F32), pltpu.VMEM((unit * n2 * n3, LANES), F32)]
        shapes += [pltpu.VMEM((n2 - 1, unit * n3, LANES), F32), pltpu.VMEM((unit * n3, LANES), F32)]
        shapes += [pltpu.VMEM((n3 - 1, unit, LANES), F32)]
    return shapes

def pick_kernel(mine, tiles, panel, q):
    t = tiles[pl.program_id(0)] - lax.axis_index("wide") * mine
    held = (t >= 0) & (t < mine)
    for cb in range(q.shape[0]):
        q[cb] = jnp.where(held, panel[:, cb * LANES:(cb + 1) * LANES], 0.0)


def pick_call(panel, tiles, tile):
    m, n = panel.shape
    mine, count = m // tile, tiles.shape[0]

    def place(i, t):
        return jnp.clip(t[i] - lax.axis_index("wide") * mine, 0, mine - 1), 0

    return pl.pallas_call(
        functools.partial(pick_kernel, mine),
        out_shape=jax.ShapeDtypeStruct((n // LANES, count * tile, LANES), F32),
        grid_spec=pltpu.PrefetchScalarGridSpec(
            num_scalar_prefetch=1, grid=(count,),
            in_specs=[pl.BlockSpec((tile, n), place)],
            out_specs=pl.BlockSpec((n // LANES, tile, LANES), lambda i, t: (0, i, 0)),
        ),
    )(tiles, panel)


def gather_kernel(dims, parts, d_ref, q, g_out, q_out, g, out, send, recv, *bufs):
    net = Net(dims, send, recv)
    x, z, y = net.me
    g[x, z, y] = d_ref[...]
    greet(net)
    diag = Diag(net, g)
    diag.start(2)
    fractions = []
    for i, (start, unit, order) in enumerate(parts):
        b = bufs[5 * i:5 * i + 5]
        fractions.append(Fraction(net, q, out, start, unit, order, [(b[0], b[1]), (b[2], b[3]), (b[4], None)]))
    diag.finish()
    diag.start(1)
    diag.finish()
    diag.start(0)
    diag.finish()
    g_out[...] = g[...].reshape(g_out.shape)
    for f in fractions:
        f.scatter_start(0)
    for level in range(3):
        for f in fractions:
            f.scatter_finish(level)
            if level < 2:
                f.scatter_start(level + 1)
            else:
                f.gather_start(2)
    for level in (1, 0):
        for f in fractions:
            f.gather_finish()
            f.gather_start(level)
    for f in fractions:
        f.gather_finish()
    q_out[...] = out[...]

def gather_call(dims, shares, diag, q):
    n, total = diag.shape[1], q.shape[0]
    parts = plan(dims, total, shares)
    count = sum(d - 1 for d in dims)
    sems = count * (1 + 2 * len(parts))
    V = pl.BlockSpec(memory_space=pltpu.VMEM)
    return pl.pallas_call(
        functools.partial(gather_kernel, dims, parts),
        out_shape=(jax.ShapeDtypeStruct((n, n), F32), jax.ShapeDtypeStruct((total, LANES), F32)),
        in_specs=[V, V],
        out_specs=(V, V),
        scratch_shapes=[pltpu.VMEM(dims + (diag.shape[0], n), F32), pltpu.VMEM((total, LANES), F32),
                        pltpu.SemaphoreType.DMA((sems,)), pltpu.SemaphoreType.DMA((sems,))] + scratch_for(dims, parts),
        compiler_params=pltpu.CompilerParams(collective_id=0, has_side_effects=True, vmem_limit_bytes=48 << 20),
    )(diag, q)


def split(x):
    hi = x.astype(BF16)
    return hi, (x - hi.astype(F32)).astype(BF16)

def dot3(a, b, dims):
    def one(x, y):
        return lax.dot_general(x, y, dims, preferred_element_type=F32)
    return one(a[0], b[0]) + (one(a[0], b[1]) + one(a[1], b[0]))

def middle_kernel(d_ref, q_ref, nh_ref, nl_ref, a, w):
    n = d_ref.shape[0]
    a[...] = d_ref[...]
    factor_inverse(a, w, n)
    ws = split(w[...])
    cols = q_ref.shape[0] // (n // LANES)
    step = min(cols, 512)
    for r in range(0, cols, step):
        picked = jnp.concatenate([q_ref[cb * cols + r:cb * cols + r + step, :] for cb in range(n // LANES)], axis=1)
        solved = dot3(split(picked), ws, NT)
        hi, lo = split(dot3(split(solved), ws, NN))
        nh_ref[r:r + step, :] = hi
        nl_ref[r:r + step, :] = lo

def middle_call(d, q):
    n = d.shape[0]
    cols = q.shape[0] // (n // LANES)
    V = pl.BlockSpec(memory_space=pltpu.VMEM)
    return pl.pallas_call(middle_kernel, out_shape=(jax.ShapeDtypeStruct((cols, n), BF16),) * 2,
        in_specs=[V, V], out_specs=(V, V), scratch_shapes=[pltpu.VMEM((n, n), F32)] * 2,
        compiler_params=pltpu.CompilerParams(vmem_limit_bytes=48 << 20))(d, q)

def update_kernel(tile, mask, p_ref, t_ref, nh_ref, nl_ref, o_ref):
    per = p_ref.shape[0] // tile
    first = pl.program_id(0) * per
    u = dot3(split(p_ref[...]), (nh_ref[...], nl_ref[...]), NT)
    for i in range(per):
        for j in range(t_ref.shape[1] // tile):
            r, c = slice(i * tile, (i + 1) * tile), slice(j * tile, (j + 1) * tile)
            t = t_ref[r, c]
            o_ref[r, c] = t - jnp.where(mask[first + i, j] != 0, u[r, c], 0.0)

def update_call(panel, trailing, mask, nh, nl, tile, rows=512):
    m, n = panel.shape
    cols = trailing.shape[1]
    whole = pl.BlockSpec((cols, n), lambda i: (0, 0))
    block = pl.BlockSpec((rows, cols), lambda i: (i, 0))
    return pl.pallas_call(functools.partial(update_kernel, tile),
        out_shape=jax.ShapeDtypeStruct(trailing.shape, F32), grid=(m // rows,),
        in_specs=[pl.BlockSpec(memory_space=pltpu.SMEM), pl.BlockSpec((rows, n), lambda i: (i, 0)), block, whole, whole],
        out_specs=block,
        compiler_params=pltpu.CompilerParams(vmem_limit_bytes=56 << 20))(mask, panel, trailing, nh, nl)


def shards(diag_block, panel, trailing, fill_mask, column_tiles):
    tile = trailing.shape[1] // column_tiles.shape[0]
    local = pick_call(panel, column_tiles, tile).reshape(-1, LANES)
    diag, picked = gather_call(DIMS, SHARES, diag_block, local)
    high, low = middle_call(diag, picked)
    return update_call(panel, trailing, fill_mask, high, low, tile)


def solution(mesh):
    return jax.shard_map(
        shards,
        mesh=mesh,
        in_specs=(P("wide", None), P("wide", None), P("wide", "loop"), P("wide", "loop"), P("loop")),
        out_specs=P("wide", "loop"),
        check_vma=False,
    )
```

```python
import functools
import math

import jax
import jax.numpy as jnp
from jax import lax
from jax.experimental import pallas as pl
from jax.experimental.pallas import tpu as pltpu
from jax.sharding import PartitionSpec as P

F32, BF16 = jnp.float32, jnp.bfloat16
HI = lax.Precision.HIGHEST
MESH = pl.DeviceIdType.MESH
SUB, WIDE, LANES = 8, 128, 128
NT = (((1,), (1,)), ((), ()))
NN = (((1,), (0,)), ((), ()))
DIMS = (4, 8, 2)
HOOKS = {20: 6, 32: 6, 40: 6, 46: 6, 54: 6}
SHARES = (((0, 1, 2), 3), ((2, 0, 1), 3), ((1, 0, 2), 2))


def lane_bcast(x, lane):
    return jnp.broadcast_to(x[:, lane:lane + 1], (SUB, WIDE))

def sub_bcast(x, row):
    return jnp.broadcast_to(x[row:row + 1, :], (SUB, WIDE))

def factor_tile(rows, hook):
    lane = lax.broadcasted_iota(jnp.int32, (SUB, WIDE), 1)
    sub = lax.broadcasted_iota(jnp.int32, (SUB, WIDE), 0)
    rows = list(rows)
    count = len(rows)
    scales = []
    for k in range(count):
        base = SUB * k
        here = (lane >= base) & (lane < base + SUB)
        own = rows[k]
        cols = [lane_bcast(own, base + p) for p in range(SUB)]
        own = jnp.where(here, jnp.where(lane - base == sub, 1.0, 0.0), own)
        invs, tops, edges = [], [], {}
        scale = jnp.ones((SUB, WIDE), F32)
        for p in range(SUB):
            inv = 1.0 / sub_bcast(cols[p], p)
            invs.append(inv)
            scale = jnp.where(sub == p, inv, scale)
            top = sub_bcast(own, p)
            tops.append(top)
            if p < SUB - 1:
                mult = jnp.where(sub > p, cols[p] * inv, 0.0)
                for q in range(p + 1, SUB):
                    edges[p, q] = sub_bcast(cols[q], p)
                    cols[q] = cols[q] - mult * edges[p, q]
                own = own - mult * top
        rows[k] = own
        scales.append(scale)
        for i in range(k + 1, count):
            below = [lane_bcast(rows[i], base + p) for p in range(SUB)]
            new = jnp.where(here, 0.0, rows[i])
            for p in range(SUB):
                mult = below[p] * invs[p]
                for q in range(p + 1, SUB):
                    below[q] = below[q] - mult * edges[p, q]
                new = new - mult * tops[p]
            rows[i] = new
        hook()
    return rows, scales

def factor_inverse(block, a, w, hook):
    n = a.shape[0]
    tiles = n // WIDE
    lane = lax.broadcasted_iota(jnp.int32, (WIDE, WIDE), 1)
    sub = lax.broadcasted_iota(jnp.int32, (WIDE, WIDE), 0)
    w[...] = jnp.zeros_like(w)
    for j in range(tiles):
        lo, hi = j * WIDE, (j + 1) * WIDE
        block(j)
        rows = [a[lo + SUB * k: lo + SUB * (k + 1), lo:hi] for k in range(WIDE // SUB)]
        rows, scales = factor_tile(rows, lambda: hook(j))
        linv = jnp.where(lane <= sub, jnp.concatenate(rows, axis=0), 0.0)
        inv = jnp.concatenate(scales, axis=0)
        root = jnp.sqrt(inv)
        w[lo:hi, lo:hi] = linv * root
        if j + 1 < tiles:
            right = jnp.dot(linv, a[lo:hi, hi:], precision=HI, preferred_element_type=F32)
            mult = lax.dot_general(a[hi:, lo:hi], linv, NT, precision=HI, preferred_element_type=F32)
        if j:
            left = jnp.dot(linv, a[lo:hi, :lo], precision=HI, preferred_element_type=F32)
            w[lo:hi, :lo] = left * jnp.concatenate([root] * j, axis=1)
        if j + 1 < tiles:
            scaled = right * jnp.concatenate([inv] * (tiles - 1 - j), axis=1)
            a[hi:, hi:] = a[hi:, hi:] - jnp.dot(mult, scaled, precision=HI, preferred_element_type=F32)
            a[hi:, lo:hi] = -jnp.dot(mult, linv * inv, precision=HI, preferred_element_type=F32)
            if j:
                scaled = left * jnp.concatenate([inv] * j, axis=1)
                a[hi:, :lo] = a[hi:, :lo] - jnp.dot(mult, scaled, precision=HI, preferred_element_type=F32)


class Net:
    def __init__(self, dims, send, recv):
        self.dims = dims
        me = lax.axis_index("wide")
        nx, nz, ny = dims
        self.me = (me // (nz * ny), (me // ny) % nz, me % ny)
        self.send, self.recv, self.used = send, recv, 0

    def peer(self, axis, step):
        c = list(self.me)
        c[axis] = lax.rem(c[axis] + step, self.dims[axis])
        return c[axis], (c[0] * self.dims[1] + c[1]) * self.dims[2] + c[2]

    def copy(self, src, dst, wide):
        i = self.used
        self.used += 1
        c = pltpu.make_async_remote_copy(src_ref=src, dst_ref=dst, send_sem=self.send.at[i], recv_sem=self.recv.at[i],
                                         device_id={"wide": wide}, device_id_type=MESH)
        c.start()
        return c

def greet(net):
    barrier = pltpu.get_barrier_semaphore()
    total = 0
    for axis in range(3):
        for step in range(1, net.dims[axis]):
            pl.semaphore_signal(barrier, inc=1, device_id={"wide": net.peer(axis, step)[1]}, device_id_type=MESH)
            total += 1
    pl.semaphore_wait(barrier, total)

class Fraction:
    def __init__(self, net, q, out, start, unit, order, bufs):
        self.net, self.q, self.out, self.start, self.order = net, q, out, start, order
        self.sizes = [net.dims[a] for a in order]
        self.coords = [net.me[a] for a in order]
        n1, n2, n3 = self.sizes
        self.blocks = [unit * n2 * n3, unit * n3, unit]
        self.bufs = bufs
        self.pending = []

    def scatter_start(self, level):
        size = self.blocks[level]
        src, base = (self.q, self.start) if level == 0 else (self.bufs[level - 1][1], 0)
        self.pending = []
        for step in range(1, self.sizes[level]):
            at, wide = self.net.peer(self.order[level], step)
            rows = pl.ds(pl.multiple_of(base + at * size, 8), size)
            self.pending.append(self.net.copy(src.at[rows], self.bufs[level][0].at[step - 1], wide))

    def scatter_finish(self, level):
        size = self.blocks[level]
        src, base = (self.q, self.start) if level == 0 else (self.bufs[level - 1][1], 0)
        for c in self.pending:
            c.wait()
        got, total = self.bufs[level]
        acc = src[pl.ds(pl.multiple_of(base + self.coords[level] * size, 8), size), :]
        for step in range(1, self.sizes[level]):
            acc = acc + got[step - 1]
        if level < 2:
            total[...] = acc
        else:
            self.out[pl.ds(self.offset(2), size), :] = acc

    def offset(self, level):
        at = self.start
        for l in range(level + 1):
            at = at + self.coords[l] * self.blocks[l]
        return pl.multiple_of(at, 8)

    def gather_start(self, level):
        rows = pl.ds(self.offset(level), self.blocks[level])
        self.pending = []
        for step in range(1, self.sizes[level]):
            _, wide = self.net.peer(self.order[level], step)
            self.pending.append(self.net.copy(self.out.at[rows], self.out.at[rows], wide))

    def gather_finish(self):
        for c in self.pending:
            c.wait()

class Diag:
    def __init__(self, net, g):
        self.net, self.g, self.pending = net, g, []

    def view(self, axis):
        x, z, y = self.net.me
        return self.g.at[x, z, y] if axis == 2 else self.g.at[x, z] if axis == 1 else self.g.at[x]

    def start(self, axis):
        self.pending = []
        for step in range(1, self.net.dims[axis]):
            _, wide = self.net.peer(axis, step)
            self.pending.append(self.net.copy(self.view(axis), self.view(axis), wide))

    def finish(self):
        for c in self.pending:
            c.wait()

def plan(dims, total, shares):
    devices = math.prod(dims)
    units = total // (8 * devices)
    out, start = [], 0
    for order, share in shares:
        unit = 8 * share
        out.append((start, unit, order))
        start += unit * devices
    assert start == total
    return out

def scratch_for(dims, parts):
    shapes = []
    for start, unit, order in parts:
        n1, n2, n3 = [dims[a] for a in order]
        shapes += [pltpu.VMEM((n1 - 1, unit * n2 * n3, LANES), F32), pltpu.VMEM((unit * n2 * n3, LANES), F32)]
        shapes += [pltpu.VMEM((n2 - 1, unit * n3, LANES), F32), pltpu.VMEM((unit * n3, LANES), F32)]
        shapes += [pltpu.VMEM((n3 - 1, unit, LANES), F32)]
    return shapes

def split(x):
    hi = x.astype(BF16)
    return hi, (x - hi.astype(F32)).astype(BF16)

def dot3(a, b, dims):
    def one(x, y):
        return lax.dot_general(x, y, dims, preferred_element_type=F32)
    return one(a[0], b[0]) + (one(a[0], b[1]) + one(a[1], b[0]))

def select_rows(panel, tiles, q, tile):
    mine = panel.shape[0] // tile
    count = tiles.shape[0]
    first = lax.axis_index("wide") * mine
    wanted = [jnp.full((SUB, LANES), tiles[c] - first, jnp.int32) for c in range(count)]

    def step(r, carry):
        for cb in range(panel.shape[1] // LANES):
            picked = [jnp.zeros((SUB, LANES), F32)] * count
            for i in range(mine):
                block = panel[pl.ds(pl.multiple_of(i * tile + r * SUB, SUB), SUB), cb * LANES:(cb + 1) * LANES]
                picked = [jnp.where(w == i, block, p) for w, p in zip(wanted, picked)]
            for c in range(count):
                q[pl.ds(pl.multiple_of((cb * count + c) * tile + r * SUB, SUB), SUB), :] = picked[c]
        return carry

    lax.fori_loop(0, tile // SUB, step, 0)


def front_kernel(dims, parts, tile, d_ref, panel_hbm, tiles, nh_ref, nl_ref, panel, q, g, a, w, out, local, send, recv, *bufs):
    net = Net(dims, send, recv)
    x, z, y = net.me
    load = pltpu.make_async_copy(panel_hbm, panel, local)
    load.start()
    g[x, z, y] = d_ref[...]
    greet(net)
    diag = Diag(net, g)
    diag.start(2)
    load.wait()
    select_rows(panel, tiles, q, tile)
    diag.finish()
    diag.start(1)
    fractions = []
    for i, (start, unit, order) in enumerate(parts):
        b = bufs[5 * i:5 * i + 5]
        fractions.append(Fraction(net, q, out, start, unit, order, [(b[0], b[1]), (b[2], b[3]), (b[4], None)]))
    diag.finish()
    diag.start(0)
    for f in fractions:
        f.scatter_start(0)

    steps = []
    for level in range(3):
        for f in fractions:
            steps.append(functools.partial(f.scatter_finish, level))
            steps.append(functools.partial(f.scatter_start, level + 1) if level < 2 else functools.partial(f.gather_start, 2))
    for level in (1, 0):
        for f in fractions:
            steps.append(f.gather_finish)
            steps.append(functools.partial(f.gather_start, level))
    for f in fractions:
        steps.append(f.gather_finish)
    calls = [0]

    def hook(j):
        at = HOOKS.get(calls[0])
        calls[0] += 1
        for _ in range(at or 0):
            steps.pop(0)()

    n = a.shape[0]

    def block(j):
        if j == 0:
            diag.finish()
            a[...] = g[...].reshape(n, n)

    factor_inverse(block, a, w, hook)
    while steps:
        steps.pop(0)()
    ws = split(w[...])
    cols = out.shape[0] // (n // LANES)
    step = min(cols, 512)
    for r in range(0, cols, step):
        picked = jnp.concatenate([out[cb * cols + r:cb * cols + r + step, :] for cb in range(n // LANES)], axis=1)
        solved = dot3(split(picked), ws, NT)
        hi, lo = split(dot3(split(solved), ws, NN))
        nh_ref[r:r + step, :] = hi
        nl_ref[r:r + step, :] = lo


def front_call(dims, shares, tile, diag, panel, tiles):
    n, cols = panel.shape[1], tiles.shape[0] * tile
    total = cols * (n // LANES)
    parts = plan(dims, total, shares)
    sems = sum(d - 1 for d in dims) * (1 + 2 * len(parts))
    V = pl.BlockSpec(memory_space=pltpu.VMEM)
    return pl.pallas_call(
        functools.partial(front_kernel, dims, parts, tile),
        out_shape=(jax.ShapeDtypeStruct((cols, n), BF16),) * 2,
        in_specs=[V, pl.BlockSpec(memory_space=pl.ANY), pl.BlockSpec(memory_space=pltpu.SMEM)],
        out_specs=(V, V),
        scratch_shapes=[pltpu.VMEM(panel.shape, F32), pltpu.VMEM((total, LANES), F32), pltpu.VMEM(dims + (diag.shape[0], n), F32),
                        pltpu.VMEM((n, n), F32), pltpu.VMEM((n, n), F32), pltpu.VMEM((total, LANES), F32), pltpu.SemaphoreType.DMA,
                        pltpu.SemaphoreType.DMA((sems,)), pltpu.SemaphoreType.DMA((sems,))] + scratch_for(dims, parts),
        compiler_params=pltpu.CompilerParams(collective_id=0, has_side_effects=True, vmem_limit_bytes=56 << 20),
    )(diag, panel, tiles)


def update_kernel(tile, mask, p_ref, t_ref, nh_ref, nl_ref, o_ref):
    per = p_ref.shape[0] // tile
    first = pl.program_id(0) * per
    u = dot3(split(p_ref[...]), (nh_ref[...], nl_ref[...]), NT)
    for i in range(per):
        for j in range(t_ref.shape[1] // tile):
            r, c = slice(i * tile, (i + 1) * tile), slice(j * tile, (j + 1) * tile)
            t = t_ref[r, c]
            o_ref[r, c] = t - jnp.where(mask[first + i, j] != 0, u[r, c], 0.0)

def update_call(panel, trailing, mask, nh, nl, tile, rows=512):
    m, n = panel.shape
    cols = trailing.shape[1]
    whole = pl.BlockSpec((cols, n), lambda i: (0, 0))
    block = pl.BlockSpec((rows, cols), lambda i: (i, 0))
    return pl.pallas_call(functools.partial(update_kernel, tile),
        out_shape=jax.ShapeDtypeStruct(trailing.shape, F32), grid=(m // rows,),
        in_specs=[pl.BlockSpec(memory_space=pltpu.SMEM), pl.BlockSpec((rows, n), lambda i: (i, 0)), block, whole, whole],
        out_specs=block,
        compiler_params=pltpu.CompilerParams(vmem_limit_bytes=56 << 20))(mask, panel, trailing, nh, nl)


def shards(diag_block, panel, trailing, fill_mask, column_tiles):
    tile = trailing.shape[1] // column_tiles.shape[0]
    high, low = front_call(DIMS, SHARES, tile, diag_block, panel, column_tiles)
    return update_call(panel, trailing, fill_mask, high, low, tile)


def solution(mesh):
    return jax.shard_map(
        shards,
        mesh=mesh,
        in_specs=(P("wide", None), P("wide", None), P("wide", "loop"), P("wide", "loop"), P("loop")),
        out_specs=P("wide", "loop"),
        check_vma=False,
    )
```

```python
import functools
import math

import jax
import jax.numpy as jnp
from jax import lax
from jax.experimental import pallas as pl
from jax.experimental.pallas import tpu as pltpu
from jax.sharding import PartitionSpec as P

F32, BF16 = jnp.float32, jnp.bfloat16
HI = lax.Precision.HIGHEST
MESH = pl.DeviceIdType.MESH
SUB, WIDE, LANES = 8, 128, 128
NT = (((1,), (1,)), ((), ()))
NN = (((1,), (0,)), ((), ()))
DIMS = (4, 8, 2)
ORDERS = (
    (0, 2, 1),
    (2, 0, 1),
    (2, 0, 1),
    (1, 0, 2),
    (0, 2, 1),
    (1, 0, 2),
    (2, 0, 1),
    (2, 0, 1),
)
BEFORE = (1, 0, -1, 2, 4, 1, 3, 6)
LATER = (
    (0, 7), (0, 2), (0, 0), (0, 3), (0, 4), (3, 6), (3, 5), (5, 1),
    (7, 3), (9, 7), (10, 2), (12, 0), (13, 5), (14, 4), (14, 3), (16, 6),
    (18, 1), (21, 5), (21, 7), (23, 2), (24, 3), (25, 0), (27, 4), (29, 5),
    (29, 6), (30, 1), (34, 7), (35, 0), (36, 2), (37, 4), (38, 5), (42, 6),
    (46, 1), (46, 7), (50, 3), (53, 2), (54, 0), (61, 6), (61, 4), (65, 5),
    (69, 7),
)


def lane_bcast(x, lane):
    return jnp.broadcast_to(x[:, lane:lane + 1], (SUB, WIDE))

def sub_bcast(x, row):
    return jnp.broadcast_to(x[row:row + 1, :], (SUB, WIDE))

def factor_tile(rows, hook):
    lane = lax.broadcasted_iota(jnp.int32, (SUB, WIDE), 1)
    sub = lax.broadcasted_iota(jnp.int32, (SUB, WIDE), 0)
    rows = list(rows)
    count = len(rows)
    scales = []
    for k in range(count):
        base = SUB * k
        here = (lane >= base) & (lane < base + SUB)
        own = rows[k]
        cols = [lane_bcast(own, base + p) for p in range(SUB)]
        own = jnp.where(here, jnp.where(lane - base == sub, 1.0, 0.0), own)
        invs, tops, edges = [], [], {}
        scale = jnp.ones((SUB, WIDE), F32)
        for p in range(SUB):
            inv = 1.0 / sub_bcast(cols[p], p)
            invs.append(inv)
            scale = jnp.where(sub == p, inv, scale)
            top = sub_bcast(own, p)
            tops.append(top)
            if p < SUB - 1:
                mult = jnp.where(sub > p, cols[p] * inv, 0.0)
                for q in range(p + 1, SUB):
                    edges[p, q] = sub_bcast(cols[q], p)
                    cols[q] = cols[q] - mult * edges[p, q]
                own = own - mult * top
        rows[k] = own
        scales.append(scale)
        for i in range(k + 1, count):
            below = [lane_bcast(rows[i], base + p) for p in range(SUB)]
            new = jnp.where(here, 0.0, rows[i])
            for p in range(SUB):
                mult = below[p] * invs[p]
                for q in range(p + 1, SUB):
                    below[q] = below[q] - mult * edges[p, q]
                new = new - mult * tops[p]
            rows[i] = new
        hook()
    return rows, scales

def factor_inverse(a, w, hook):
    n = a.shape[0]
    tiles = n // WIDE
    lane = lax.broadcasted_iota(jnp.int32, (WIDE, WIDE), 1)
    sub = lax.broadcasted_iota(jnp.int32, (WIDE, WIDE), 0)
    w[...] = jnp.zeros_like(w)
    for j in range(tiles):
        lo, hi = j * WIDE, (j + 1) * WIDE
        rows = [a[lo + SUB * k: lo + SUB * (k + 1), lo:hi] for k in range(WIDE // SUB)]
        rows, scales = factor_tile(rows, hook)
        linv = jnp.where(lane <= sub, jnp.concatenate(rows, axis=0), 0.0)
        inv = jnp.concatenate(scales, axis=0)
        root = jnp.sqrt(inv)
        w[lo:hi, lo:hi] = linv * root
        if j + 1 < tiles:
            right = jnp.dot(linv, a[lo:hi, hi:], precision=HI, preferred_element_type=F32)
            mult = lax.dot_general(a[hi:, lo:hi], linv, NT, precision=HI, preferred_element_type=F32)
        if j:
            left = jnp.dot(linv, a[lo:hi, :lo], precision=HI, preferred_element_type=F32)
            w[lo:hi, :lo] = left * jnp.concatenate([root] * j, axis=1)
        if j + 1 < tiles:
            scaled = right * jnp.concatenate([inv] * (tiles - 1 - j), axis=1)
            a[hi:, hi:] = a[hi:, hi:] - jnp.dot(mult, scaled, precision=HI, preferred_element_type=F32)
            a[hi:, lo:hi] = -jnp.dot(mult, linv * inv, precision=HI, preferred_element_type=F32)
            if j:
                scaled = left * jnp.concatenate([inv] * j, axis=1)
                a[hi:, :lo] = a[hi:, :lo] - jnp.dot(mult, scaled, precision=HI, preferred_element_type=F32)


class Net:
    def __init__(self, dims, send, recv):
        self.dims = dims
        me = lax.axis_index("wide")
        nx, nz, ny = dims
        self.me = (me // (nz * ny), (me // ny) % nz, me % ny)
        loop = lax.axis_index("loop")
        self.core = lax.rem(loop, 2)
        self.twin = {"loop": loop + 1 - 2 * self.core}
        self.send, self.recv, self.used, self.sent = send, recv, 0, []

    def peer(self, steps):
        c = [lax.rem(c + s, n) for c, s, n in zip(self.me, steps, self.dims)]
        return c, {"wide": (c[0] * self.dims[1] + c[1]) * self.dims[2] + c[2]}

    def along(self, axis, step):
        c, device = self.peer([step if a == axis else 0 for a in range(3)])
        return c[axis], device

    def plane(self):
        steps = [(0, dz, dy) for dz in range(self.dims[1]) for dy in range(self.dims[2]) if dz or dy]
        return sorted(steps, key=lambda s: -min(s[1], self.dims[1] - s[1]) - s[2])

    def slot(self):
        self.used += 1
        return self.used - 1

    def copy(self, src, dst, device, slot):
        pltpu.make_async_remote_copy(
            src_ref=src, dst_ref=dst, send_sem=self.send.at[slot], recv_sem=self.recv.at[slot], device_id=device, device_id_type=MESH
        ).start()

    def arrived(self, like, slot):
        pltpu.make_async_copy(like, like, self.recv.at[slot]).wait()
        self.sent.append((like, slot))

    def drain(self):
        for like, slot in self.sent:
            pltpu.make_async_copy(like, like, self.send.at[slot]).wait()

    def greet(self):
        devices = [self.peer(s)[1] for s in self.plane()] + [self.along(0, s)[1] for s in range(1, self.dims[0])] + [self.twin]
        for device in devices:
            pl.semaphore_signal(pltpu.get_barrier_semaphore(), inc=1, device_id=device, device_id_type=MESH)
        return len(devices)


class Reduced:
    def __init__(self, net, q, out, start, unit, order, bufs):
        self.net, self.q, self.out, self.start, self.order = net, q, out, start, order
        self.sizes = [net.dims[a] for a in order]
        self.coords = [net.me[a] for a in order]
        n1, n2, n3 = self.sizes
        self.blocks = [unit * n2 * n3, unit * n3, unit]
        self.bufs = bufs
        self.stage = 0

    def offset(self, level):
        at = self.start
        for l in range(level + 1):
            at = at + self.coords[l] * self.blocks[l]
        return pl.multiple_of(at, SUB)

    def source(self, level):
        return (self.q, self.start) if level == 0 else (self.bufs[level - 1][1], 0)

    def begin(self):
        self.slot = self.net.slot()
        level = min(self.stage, 5 - self.stage)
        size = self.blocks[level]
        for step in range(1, self.sizes[level]):
            at, device = self.net.along(self.order[level], step)
            if self.stage < 3:
                src, base = self.source(level)
                rows = pl.ds(pl.multiple_of(base + at * size, SUB), size)
                self.net.copy(src.at[rows], self.bufs[level][0].at[pl.ds((step - 1) * size, size)], device, self.slot)
            else:
                rows = pl.ds(self.offset(level), size)
                self.net.copy(self.out.at[rows], self.out.at[rows], device, self.slot)

    def finish(self):
        level = min(self.stage, 5 - self.stage)
        size, others = self.blocks[level], self.sizes[level] - 1
        if self.stage < 3:
            got, total = self.bufs[level]
            self.net.arrived(got, self.slot)
            src, base = self.source(level)
            acc = src[pl.ds(pl.multiple_of(base + self.coords[level] * size, SUB), size), :]
            for step in range(others):
                acc = acc + got[step * size:(step + 1) * size, :]
            if level < 2:
                total[...] = acc
            else:
                self.out[pl.ds(self.offset(2), size), :] = acc
        else:
            self.net.arrived(self.out.at[pl.ds(self.start, others * size)], self.slot)
        self.stage += 1

    def advance(self):
        self.finish()
        if self.stage < 6:
            self.begin()


class Diag:
    def __init__(self, net, g, like):
        self.net, self.g, self.like = net, g, like

    def spread(self):
        x, z, y = self.net.me
        own = self.g.at[self.net.core, x, z, y]
        self.slot = self.net.slot()
        for steps in self.net.plane():
            self.net.copy(own, own, self.net.peer(steps)[1], self.slot)

    def cross(self):
        nx, nz, ny = self.net.dims
        shape = self.g.shape
        self.net.arrived(self.like.at[pl.ds(0, (nz * ny - 1) * shape[4] * shape[5] // LANES)], self.slot)
        own = self.g.at[self.net.core, self.net.me[0]]
        self.slots = [self.net.slot() for _ in range(2 * nx)]
        for step in range(1, nx):
            self.net.copy(own, own, self.net.along(0, step)[1], self.slots[step])
        self.net.copy(own, own, self.net.twin, self.slots[nx])

    def swap(self):
        nx = self.net.dims[0]
        for step in range(1, nx):
            self.net.arrived(self.g.at[0, 0], self.slots[step])
            block = self.g.at[self.net.core, lax.rem(self.net.me[0] + nx - step, nx)]
            self.net.copy(block, block, self.net.twin, self.slots[nx + step])
        for step in range(nx):
            self.net.arrived(self.g.at[0, 0], self.slots[nx + step])


def scratch_for(dims, unit, orders):
    shapes = []
    for order in orders:
        n1, n2, n3 = [dims[a] for a in order]
        for level, (n, size) in enumerate(((n1, unit * n2 * n3), (n2, unit * n3), (n3, unit))):
            shapes += [pltpu.VMEM(((n - 1) * size, LANES), F32)] + [pltpu.VMEM((size, LANES), F32)] * (level < 2)
    return shapes


def split(x):
    hi = x.astype(BF16)
    return hi, (x - hi.astype(F32)).astype(BF16)

def dot3(a, b, dims):
    def one(x, y):
        return lax.dot_general(x, y, dims, preferred_element_type=F32)
    return one(a[0], b[0]) + (one(a[0], b[1]) + one(a[1], b[0]))

def select_rows(panel, tiles, q, tile):
    mine = panel.shape[0] // tile
    count, blocks = tiles.shape[0], panel.shape[1] // LANES
    first = lax.axis_index("wide") * mine
    wanted = [jnp.full((SUB, LANES), tiles[c] - first, jnp.int32) for c in range(count)]

    def step(r, carry):
        for cb in range(blocks):
            picked = [jnp.zeros((SUB, LANES), F32)] * count
            for i in range(mine):
                block = panel[pl.ds(pl.multiple_of(i * tile + r * SUB, SUB), SUB), cb * LANES:(cb + 1) * LANES]
                picked = [jnp.where(w == i, block, p) for w, p in zip(wanted, picked)]
            for c in range(count):
                q[pl.ds(pl.multiple_of((c * blocks + cb) * tile + r * SUB, SUB), SUB), :] = picked[c]
        return carry

    lax.fori_loop(0, tile // SUB, step, 0)


def front_kernel(dims, orders, tile, d_ref, panel_hbm, tiles, nh_ref, nl_ref, panel, q, g, a, w, out, local, send, recv, *bufs):
    n = a.shape[0]
    blocks = n // LANES
    half = n // 2
    net = Net(dims, send, recv)
    load = pltpu.make_async_copy(panel_hbm, panel, local)
    load.start()
    greeted = net.greet()
    g[net.core, net.me[0], net.me[1], net.me[2]] = d_ref[:, pl.ds(pl.multiple_of(net.core * half, LANES), half)]
    load.wait()
    select_rows(panel, tiles, q, tile)
    pl.semaphore_wait(pltpu.get_barrier_semaphore(), greeted)

    diag = Diag(net, g, q)
    diag.spread()
    rows = tile * blocks
    unit = rows // math.prod(dims)
    reduced = []
    for c, order in enumerate(orders):
        b = bufs[5 * c:5 * c + 5]
        reduced.append(Reduced(net, q, out, c * rows, unit, order, [(b[0], b[1]), (b[2], b[3]), (b[4], None)]))
        reduced[c].begin()
    for c in BEFORE:
        if c < 0:
            diag.cross()
        else:
            reduced[c].advance()
    diag.swap()
    for h in range(2):
        a[:, h * half:(h + 1) * half] = g[h].reshape(n, half)

    later = list(LATER)
    calls = [0]

    def hook():
        while later and later[0][0] <= calls[0]:
            reduced[later.pop(0)[1]].advance()
        calls[0] += 1

    factor_inverse(a, w, hook)
    wt = split(w[...].T)
    inverse = split(dot3(wt, split(w[...]), NN))

    def emit(c):
        picked = jnp.concatenate([out[c * rows + cb * tile:c * rows + (cb + 1) * tile, :] for cb in range(blocks)], axis=1)
        hi, lo = split(dot3(split(picked), inverse, NN))
        nh_ref[c * tile:(c + 1) * tile, :] = hi
        nl_ref[c * tile:(c + 1) * tile, :] = lo

    for c in range(len(orders)):
        if reduced[c].stage == 6:
            emit(c)
    for _, c in later:
        reduced[c].advance()
        if reduced[c].stage == 6:
            emit(c)
    net.drain()


def front_call(dims, orders, tile, diag, panel, tiles):
    n, cols = panel.shape[1], tiles.shape[0] * tile
    total = cols * (n // LANES)
    unit = tile * (n // LANES) // math.prod(dims)
    sems = 1 + 2 * dims[0] + 6 * len(orders)
    V = pl.BlockSpec(memory_space=pltpu.VMEM)
    return pl.pallas_call(
        functools.partial(front_kernel, dims, orders, tile),
        out_shape=(jax.ShapeDtypeStruct((cols, n), BF16),) * 2,
        in_specs=[V, pl.BlockSpec(memory_space=pl.ANY), pl.BlockSpec(memory_space=pltpu.SMEM)],
        out_specs=(V, V),
        scratch_shapes=[
            pltpu.VMEM(panel.shape, F32), pltpu.VMEM((total, LANES), F32), pltpu.VMEM((2,) + dims + (diag.shape[0], n // 2), F32),
            pltpu.VMEM((n, n), F32), pltpu.VMEM((n, n), F32), pltpu.VMEM((total, LANES), F32), pltpu.SemaphoreType.DMA,
            pltpu.SemaphoreType.DMA((sems,)), pltpu.SemaphoreType.DMA((sems,)),
        ] + scratch_for(dims, unit, orders),
        compiler_params=pltpu.CompilerParams(collective_id=0, has_side_effects=True, vmem_limit_bytes=56 << 20),
    )(diag, panel, tiles)


def update_kernel(tile, mask, p_ref, t_ref, nh_ref, nl_ref, o_ref):
    per = p_ref.shape[0] // tile
    first = pl.program_id(0) * per
    u = dot3(split(p_ref[...]), (nh_ref[...], nl_ref[...]), NT)
    for i in range(per):
        for j in range(t_ref.shape[1] // tile):
            r, c = slice(i * tile, (i + 1) * tile), slice(j * tile, (j + 1) * tile)
            t = t_ref[r, c]
            o_ref[r, c] = t - jnp.where(mask[first + i, j] != 0, u[r, c], 0.0)

def update_call(panel, trailing, mask, nh, nl, tile, rows=512):
    m, n = panel.shape
    cols = trailing.shape[1]
    whole = pl.BlockSpec((cols, n), lambda i: (0, 0))
    block = pl.BlockSpec((rows, cols), lambda i: (i, 0))
    return pl.pallas_call(functools.partial(update_kernel, tile),
        out_shape=jax.ShapeDtypeStruct(trailing.shape, F32), grid=(m // rows,),
        in_specs=[pl.BlockSpec(memory_space=pltpu.SMEM), pl.BlockSpec((rows, n), lambda i: (i, 0)), block, whole, whole],
        out_specs=block,
        compiler_params=pltpu.CompilerParams(vmem_limit_bytes=56 << 20))(mask, panel, trailing, nh, nl)


def shards(diag_block, panel, trailing, fill_mask, column_tiles):
    tile = trailing.shape[1] // column_tiles.shape[0]
    high, low = front_call(DIMS, ORDERS, tile, diag_block, panel, column_tiles)
    return update_call(panel, trailing, fill_mask, high, low, tile)


def solution(mesh):
    return jax.shard_map(
        shards,
        mesh=mesh,
        in_specs=(P("wide", None), P("wide", None), P("wide", "loop"), P("wide", "loop"), P("loop")),
        out_specs=P("wide", "loop"),
        check_vma=False,
    )
```

```python
import functools
import math

import jax
import jax.numpy as jnp
from jax import lax
from jax.experimental import pallas as pl
from jax.experimental.pallas import tpu as pltpu
from jax.sharding import PartitionSpec as P

F32, BF16 = jnp.float32, jnp.bfloat16
HI = lax.Precision.HIGHEST
MESH = pl.DeviceIdType.MESH
SUB, WIDE, LANES = 8, 128, 128
NT = (((1,), (1,)), ((), ()))
NN = (((1,), (0,)), ((), ()))
DIMS = (4, 8, 2)
FRONT_VMEM, UPDATE_VMEM = 28 << 20, 24 << 20
ORDERS = (
    (0, 2, 1),
    (2, 0, 1),
    (2, 0, 1),
    (1, 0, 2),
    (0, 2, 1),
    (1, 0, 2),
    (2, 0, 1),
    (2, 0, 1),
)
BEFORE = (1, 0, -1, 2, 4, 1, 3, 6)
LATER = (
    (0, 7), (0, 2), (0, 0), (0, 3), (0, 4), (3, 6), (3, 5), (5, 1),
    (7, 3), (9, 7), (10, 2), (12, 0), (13, 5), (14, 4), (14, 3), (16, 6),
    (18, 1), (21, 5), (21, 7), (23, 2), (24, 3), (25, 0), (27, 4), (29, 5),
    (29, 6), (30, 1), (34, 7), (35, 0), (36, 2), (37, 4), (38, 5), (42, 6),
    (46, 1), (46, 7), (50, 3), (53, 2), (54, 0), (61, 6), (61, 4), (65, 5),
    (69, 7),
)


def lane_bcast(x, lane):
    return jnp.broadcast_to(x[:, lane:lane + 1], (SUB, WIDE))

def sub_bcast(x, row):
    return jnp.broadcast_to(x[row:row + 1, :], (SUB, WIDE))

def factor_tile(rows, hook):
    lane = lax.broadcasted_iota(jnp.int32, (SUB, WIDE), 1)
    sub = lax.broadcasted_iota(jnp.int32, (SUB, WIDE), 0)
    rows = list(rows)
    count = len(rows)
    scales = []
    for k in range(count):
        base = SUB * k
        here = (lane >= base) & (lane < base + SUB)
        own = rows[k]
        cols = [lane_bcast(own, base + p) for p in range(SUB)]
        own = jnp.where(here, jnp.where(lane - base == sub, 1.0, 0.0), own)
        invs, tops, edges = [], [], {}
        scale = jnp.ones((SUB, WIDE), F32)
        for p in range(SUB):
            inv = 1.0 / sub_bcast(cols[p], p)
            invs.append(inv)
            scale = jnp.where(sub == p, inv, scale)
            top = sub_bcast(own, p)
            tops.append(top)
            if p < SUB - 1:
                mult = jnp.where(sub > p, cols[p] * inv, 0.0)
                for q in range(p + 1, SUB):
                    edges[p, q] = sub_bcast(cols[q], p)
                    cols[q] = cols[q] - mult * edges[p, q]
                own = own - mult * top
        rows[k] = own
        scales.append(scale)
        for i in range(k + 1, count):
            below = [lane_bcast(rows[i], base + p) for p in range(SUB)]
            new = jnp.where(here, 0.0, rows[i])
            for p in range(SUB):
                mult = below[p] * invs[p]
                for q in range(p + 1, SUB):
                    below[q] = below[q] - mult * edges[p, q]
                new = new - mult * tops[p]
            rows[i] = new
        hook()
    return rows, scales

def factor_inverse(a, w, hook):
    n = a.shape[0]
    tiles = n // WIDE
    lane = lax.broadcasted_iota(jnp.int32, (WIDE, WIDE), 1)
    sub = lax.broadcasted_iota(jnp.int32, (WIDE, WIDE), 0)
    w[...] = jnp.zeros_like(w)
    for j in range(tiles):
        lo, hi = j * WIDE, (j + 1) * WIDE
        rows = [a[lo + SUB * k: lo + SUB * (k + 1), lo:hi] for k in range(WIDE // SUB)]
        rows, scales = factor_tile(rows, hook)
        linv = jnp.where(lane <= sub, jnp.concatenate(rows, axis=0), 0.0)
        inv = jnp.concatenate(scales, axis=0)
        root = jnp.sqrt(inv)
        w[lo:hi, lo:hi] = linv * root
        if j + 1 < tiles:
            right = jnp.dot(linv, a[lo:hi, hi:], precision=HI, preferred_element_type=F32)
            mult = lax.dot_general(a[hi:, lo:hi], linv, NT, precision=HI, preferred_element_type=F32)
        if j:
            left = jnp.dot(linv, a[lo:hi, :lo], precision=HI, preferred_element_type=F32)
            w[lo:hi, :lo] = left * jnp.concatenate([root] * j, axis=1)
        if j + 1 < tiles:
            scaled = right * jnp.concatenate([inv] * (tiles - 1 - j), axis=1)
            a[hi:, hi:] = a[hi:, hi:] - jnp.dot(mult, scaled, precision=HI, preferred_element_type=F32)
            a[hi:, lo:hi] = -jnp.dot(mult, linv * inv, precision=HI, preferred_element_type=F32)
            if j:
                scaled = left * jnp.concatenate([inv] * j, axis=1)
                a[hi:, :lo] = a[hi:, :lo] - jnp.dot(mult, scaled, precision=HI, preferred_element_type=F32)


class Net:
    def __init__(self, dims, send, recv):
        self.dims = dims
        me = lax.axis_index("wide")
        nx, nz, ny = dims
        self.me = (me // (nz * ny), (me // ny) % nz, me % ny)
        loop = lax.axis_index("loop")
        self.core = lax.rem(loop, 2)
        self.twin = {"loop": loop + 1 - 2 * self.core}
        self.send, self.recv, self.used, self.sent = send, recv, 0, []

    def peer(self, steps):
        c = [lax.rem(c + s, n) for c, s, n in zip(self.me, steps, self.dims)]
        return c, {"wide": (c[0] * self.dims[1] + c[1]) * self.dims[2] + c[2]}

    def along(self, axis, step):
        c, device = self.peer([step if a == axis else 0 for a in range(3)])
        return c[axis], device

    def plane(self):
        steps = [(0, dz, dy) for dz in range(self.dims[1]) for dy in range(self.dims[2]) if dz or dy]
        return sorted(steps, key=lambda s: -min(s[1], self.dims[1] - s[1]) - s[2])

    def slot(self):
        self.used += 1
        return self.used - 1

    def copy(self, src, dst, device, slot):
        pltpu.make_async_remote_copy(
            src_ref=src, dst_ref=dst, send_sem=self.send.at[slot], recv_sem=self.recv.at[slot], device_id=device, device_id_type=MESH
        ).start()

    def arrived(self, like, slot):
        pltpu.make_async_copy(like, like, self.recv.at[slot]).wait()
        self.sent.append((like, slot))

    def drain(self):
        for like, slot in self.sent:
            pltpu.make_async_copy(like, like, self.send.at[slot]).wait()

    def greet(self):
        devices = [self.peer(s)[1] for s in self.plane()] + [self.along(0, s)[1] for s in range(1, self.dims[0])] + [self.twin]
        for device in devices:
            pl.semaphore_signal(pltpu.get_barrier_semaphore(), inc=1, device_id=device, device_id_type=MESH)
        return len(devices)


class Reduced:
    def __init__(self, net, q, out, start, unit, order, bufs):
        self.net, self.q, self.out, self.start, self.order = net, q, out, start, order
        self.sizes = [net.dims[a] for a in order]
        self.coords = [net.me[a] for a in order]
        n1, n2, n3 = self.sizes
        self.blocks = [unit * n2 * n3, unit * n3, unit]
        self.bufs = bufs
        self.stage = 0

    def offset(self, level):
        at = self.start
        for l in range(level + 1):
            at = at + self.coords[l] * self.blocks[l]
        return pl.multiple_of(at, SUB)

    def source(self, level):
        return (self.q, self.start) if level == 0 else (self.bufs[level - 1][1], 0)

    def begin(self):
        self.slot = self.net.slot()
        level = min(self.stage, 5 - self.stage)
        size = self.blocks[level]
        for step in range(1, self.sizes[level]):
            at, device = self.net.along(self.order[level], step)
            if self.stage < 3:
                src, base = self.source(level)
                rows = pl.ds(pl.multiple_of(base + at * size, SUB), size)
                self.net.copy(src.at[rows], self.bufs[level][0].at[pl.ds((step - 1) * size, size)], device, self.slot)
            else:
                rows = pl.ds(self.offset(level), size)
                self.net.copy(self.out.at[rows], self.out.at[rows], device, self.slot)

    def finish(self):
        level = min(self.stage, 5 - self.stage)
        size, others = self.blocks[level], self.sizes[level] - 1
        if self.stage < 3:
            got, total = self.bufs[level]
            self.net.arrived(got, self.slot)
            src, base = self.source(level)
            acc = src[pl.ds(pl.multiple_of(base + self.coords[level] * size, SUB), size), :]
            for step in range(others):
                acc = acc + got[step * size:(step + 1) * size, :]
            if level < 2:
                total[...] = acc
            else:
                self.out[pl.ds(self.offset(2), size), :] = acc
        else:
            self.net.arrived(self.out.at[pl.ds(self.start, others * size)], self.slot)
        self.stage += 1

    def advance(self):
        self.finish()
        if self.stage < 6:
            self.begin()


class Diag:
    def __init__(self, net, g, like):
        self.net, self.g, self.like = net, g, like

    def spread(self):
        x, z, y = self.net.me
        own = self.g.at[self.net.core, x, z, y]
        self.slot = self.net.slot()
        for steps in self.net.plane():
            self.net.copy(own, own, self.net.peer(steps)[1], self.slot)

    def cross(self):
        nx, nz, ny = self.net.dims
        shape = self.g.shape
        self.net.arrived(self.like.at[pl.ds(0, (nz * ny - 1) * shape[4] * shape[5] // LANES)], self.slot)
        own = self.g.at[self.net.core, self.net.me[0]]
        self.slots = [self.net.slot() for _ in range(2 * nx)]
        for step in range(1, nx):
            self.net.copy(own, own, self.net.along(0, step)[1], self.slots[step])
        self.net.copy(own, own, self.net.twin, self.slots[nx])

    def swap(self):
        nx = self.net.dims[0]
        for step in range(1, nx):
            self.net.arrived(self.g.at[0, 0], self.slots[step])
            block = self.g.at[self.net.core, lax.rem(self.net.me[0] + nx - step, nx)]
            self.net.copy(block, block, self.net.twin, self.slots[nx + step])
        for step in range(nx):
            self.net.arrived(self.g.at[0, 0], self.slots[nx + step])


def scratch_for(dims, unit, orders):
    shapes = []
    for order in orders:
        n1, n2, n3 = [dims[a] for a in order]
        for level, (n, size) in enumerate(((n1, unit * n2 * n3), (n2, unit * n3), (n3, unit))):
            shapes += [pltpu.VMEM(((n - 1) * size, LANES), F32)] + [pltpu.VMEM((size, LANES), F32)] * (level < 2)
    return shapes


def split(x):
    hi = x.astype(BF16)
    return hi, (x - hi.astype(F32)).astype(BF16)

def dot3(a, b, dims):
    def one(x, y):
        return lax.dot_general(x, y, dims, preferred_element_type=F32)
    return one(a[0], b[0]) + (one(a[0], b[1]) + one(a[1], b[0]))

def select_rows(panel, tiles, q, tile):
    mine = panel.shape[0] // tile
    count, blocks = tiles.shape[0], panel.shape[1] // LANES
    first = lax.axis_index("wide") * mine
    wanted = [jnp.full((SUB, LANES), tiles[c] - first, jnp.int32) for c in range(count)]

    def step(r, carry):
        for cb in range(blocks):
            picked = [jnp.zeros((SUB, LANES), F32)] * count
            for i in range(mine):
                block = panel[pl.ds(pl.multiple_of(i * tile + r * SUB, SUB), SUB), cb * LANES:(cb + 1) * LANES]
                picked = [jnp.where(w == i, block, p) for w, p in zip(wanted, picked)]
            for c in range(count):
                q[pl.ds(pl.multiple_of((c * blocks + cb) * tile + r * SUB, SUB), SUB), :] = picked[c]
        return carry

    lax.fori_loop(0, tile // SUB, step, 0)


def front_kernel(dims, orders, tile, d_ref, panel_hbm, t_in, tiles, nh_ref, nl_ref, ph_ref, pl_ref, t_out, panel, q, g, a, w, out, local, send, recv, *bufs):
    n = a.shape[0]
    blocks = n // LANES
    half = n // 2
    net = Net(dims, send, recv)
    load = pltpu.make_async_copy(panel_hbm, panel, local.at[0])
    load.start()
    hand = pltpu.make_async_copy(t_in, t_out, local.at[1])
    hand.start()
    greeted = net.greet()
    g[net.core, net.me[0], net.me[1], net.me[2]] = d_ref[:, pl.ds(pl.multiple_of(net.core * half, LANES), half)]
    load.wait()
    select_rows(panel, tiles, q, tile)
    pl.semaphore_wait(pltpu.get_barrier_semaphore(), greeted)

    diag = Diag(net, g, q)
    diag.spread()
    rows = tile * blocks
    unit = rows // math.prod(dims)
    reduced = []
    for c, order in enumerate(orders):
        b = bufs[5 * c:5 * c + 5]
        reduced.append(Reduced(net, q, out, c * rows, unit, order, [(b[0], b[1]), (b[2], b[3]), (b[4], None)]))
        reduced[c].begin()
    for c in BEFORE:
        if c < 0:
            diag.cross()
        else:
            reduced[c].advance()

    def parts(r, carry):
        rows = pl.ds(pl.multiple_of(r * tile, tile), tile)
        ph_ref[rows, :], pl_ref[rows, :] = split(panel[rows, :])
        return carry

    lax.fori_loop(0, panel.shape[0] // tile, parts, 0)
    diag.swap()
    for h in range(2):
        a[:, h * half:(h + 1) * half] = g[h].reshape(n, half)

    later = list(LATER)
    calls = [0]

    def hook():
        while later and later[0][0] <= calls[0]:
            reduced[later.pop(0)[1]].advance()
        calls[0] += 1

    factor_inverse(a, w, hook)
    wt = split(w[...].T)
    inverse = split(dot3(wt, split(w[...]), NN))

    def emit(group):
        picked = [jnp.concatenate([out[c * rows + cb * tile:c * rows + (cb + 1) * tile, :] for cb in range(blocks)], axis=1) for c in group]
        hi, lo = split(dot3(split(jnp.concatenate(picked, axis=0)), inverse, NN))
        for i, c in enumerate(group):
            nh_ref[c * tile:(c + 1) * tile, :] = hi[i * tile:(i + 1) * tile]
            nl_ref[c * tile:(c + 1) * tile, :] = lo[i * tile:(i + 1) * tile]

    ended = [c for c in range(len(orders)) if reduced[c].stage == 6]
    for _, c in later:
        if len(ended) >= 2:
            emit(ended)
            ended = []
        reduced[c].advance()
        if reduced[c].stage == 6:
            ended.append(c)
    emit(ended)
    hand.wait()
    net.drain()


def front_call(dims, orders, tile, diag, panel, trailing, tiles):
    n, cols = panel.shape[1], tiles.shape[0] * tile
    total = cols * (n // LANES)
    unit = tile * (n // LANES) // math.prod(dims)
    sems = 1 + 2 * dims[0] + 6 * len(orders)
    V = pl.BlockSpec(memory_space=pltpu.VMEM)
    A = pl.BlockSpec(memory_space=pl.ANY)
    H = pl.BlockSpec(memory_space=pltpu.HBM)
    return pl.pallas_call(
        functools.partial(front_kernel, dims, orders, tile),
        out_shape=(jax.ShapeDtypeStruct((cols, n), BF16),) * 2 + (jax.ShapeDtypeStruct(panel.shape, BF16),) * 2 + (jax.ShapeDtypeStruct(trailing.shape, F32),),
        in_specs=[V, H, H, pl.BlockSpec(memory_space=pltpu.SMEM)],
        out_specs=(V, V, V, V, A),
        scratch_shapes=[
            pltpu.VMEM(panel.shape, F32), pltpu.VMEM((total, LANES), F32), pltpu.VMEM((2,) + dims + (diag.shape[0], n // 2), F32),
            pltpu.VMEM((n, n), F32), pltpu.VMEM((n, n), F32), pltpu.VMEM((total, LANES), F32), pltpu.SemaphoreType.DMA((2,)),
            pltpu.SemaphoreType.DMA((sems,)), pltpu.SemaphoreType.DMA((sems,)),
        ] + scratch_for(dims, unit, orders),
        cost_estimate=pl.CostEstimate(flops=10 * n**3, bytes_accessed=200_000_000, transcendentals=0),
        compiler_params=pltpu.CompilerParams(collective_id=0, has_side_effects=True, vmem_limit_bytes=FRONT_VMEM),
    )(diag, panel, trailing, tiles)


def update_kernel(tile, rows, mask, ph_ref, pl_ref, t_ref, nh_ref, nl_ref, o_hbm, o, sems):
    steps = t_ref.shape[0] // rows

    def part(k):
        return pl.ds(pl.multiple_of(k * rows, rows), rows)

    def step(k, carry):
        u = dot3((ph_ref[part(k), :], pl_ref[part(k), :]), (nh_ref[...], nl_ref[...]), NT)
        for i in range(rows // tile):
            r = pl.ds(pl.multiple_of(k * rows + i * tile, tile), tile)
            for j in range(t_ref.shape[1] // tile):
                c = slice(j * tile, (j + 1) * tile)
                filled = mask[j, k * (rows // tile) + i] != 0
                o[r, c] = t_ref[r, c] - jnp.where(filled, u[i * tile:(i + 1) * tile, c], 0.0)
        pltpu.make_async_copy(o.at[part(k)], o_hbm.at[part(k)], sems.at[k]).start()
        return carry

    lax.fori_loop(0, steps, step, 0)
    for k in range(steps):
        pltpu.make_async_copy(o.at[part(k)], o_hbm.at[part(k)], sems.at[k]).wait()


def update_call(ph, pl_, trailing, mask, nh, nl, tile, rows=512):
    V = pl.BlockSpec(memory_space=pltpu.VMEM)
    return pl.pallas_call(
        functools.partial(update_kernel, tile, rows),
        out_shape=jax.ShapeDtypeStruct(trailing.shape, F32),
        in_specs=[pl.BlockSpec(memory_space=pltpu.SMEM), V, V, V, V, V],
        out_specs=pl.BlockSpec(memory_space=pl.ANY),
        scratch_shapes=[pltpu.VMEM(trailing.shape, F32), pltpu.SemaphoreType.DMA((trailing.shape[0] // rows,))],
        compiler_params=pltpu.CompilerParams(vmem_limit_bytes=UPDATE_VMEM),
    )(mask, ph, pl_, trailing, nh, nl)


def shards(diag_block, panel, trailing, fill_mask, column_tiles):
    tile = trailing.shape[1] // column_tiles.shape[0]
    far = [pltpu.with_memory_space_constraint(x, pltpu.HBM) for x in (diag_block, panel, trailing, column_tiles)]
    high, low, panel_high, panel_low, kept = front_call(DIMS, ORDERS, tile, *far)
    return update_call(panel_high, panel_low, kept, fill_mask.T, high, low, tile)


def solution(mesh):
    return jax.shard_map(
        shards,
        mesh=mesh,
        in_specs=(P("wide", None), P("wide", None), P("wide", "loop"), P("wide", "loop"), P("loop")),
        out_specs=P("wide", "loop"),
        check_vma=False,
    )
```

```python
import functools
import math

import jax
import jax.numpy as jnp
from jax import lax
from jax.experimental import pallas as pl
from jax.experimental.pallas import tpu as pltpu
from jax.sharding import PartitionSpec as P

F32, BF16 = jnp.float32, jnp.bfloat16
HI = lax.Precision.HIGHEST
MESH = pl.DeviceIdType.MESH
SUB, WIDE, LANES = 8, 128, 128
NT = (((1,), (1,)), ((), ()))
NN = (((1,), (0,)), ((), ()))
DIMS = (4, 8, 2)
FRONT_VMEM, UPDATE_VMEM = 28 << 20, 24 << 20
ORDERS = (
    (0, 2, 1),
    (2, 0, 1),
    (2, 0, 1),
    (1, 0, 2),
    (0, 2, 1),
    (2, 0, 1),
    (1, 0, 2),
    (2, 0, 1),
)
BEFORE = (1, 0, -1, 2, 4, 1, 3, 5)
LATER = (
    (0, 7), (0, 2), (0, 0), (0, 3), (0, 4), (3, 5), (3, 6), (5, 1),
    (7, 3), (9, 7), (10, 2), (12, 0), (13, 6), (14, 4), (14, 3), (16, 5),
    (18, 1), (21, 6), (21, 7), (23, 2), (24, 3), (25, 0), (27, 4), (29, 6),
    (29, 5), (30, 1), (34, 7), (35, 0), (36, 2), (37, 4), (38, 6), (42, 5),
    (46, 7),
)
GROUPS = ((1, 3, 2, 0), (5, 4), (6, 7))


def lane_bcast(x, lane):
    return jnp.broadcast_to(x[:, lane:lane + 1], (SUB, WIDE))

def sub_bcast(x, row):
    return jnp.broadcast_to(x[row:row + 1, :], (SUB, WIDE))

def factor_tile(rows, hook):
    lane = lax.broadcasted_iota(jnp.int32, (SUB, WIDE), 1)
    sub = lax.broadcasted_iota(jnp.int32, (SUB, WIDE), 0)
    rows = list(rows)
    count = len(rows)
    scales = []
    for k in range(count):
        base = SUB * k
        here = (lane >= base) & (lane < base + SUB)
        own = rows[k]
        cols = [lane_bcast(own, base + p) for p in range(SUB)]
        own = jnp.where(here, jnp.where(lane - base == sub, 1.0, 0.0), own)
        invs, tops, edges = [], [], {}
        scale = jnp.ones((SUB, WIDE), F32)
        pivot = sub_bcast(cols[0], 0)
        for p in range(SUB):
            inv = 1.0 / pivot
            if p < SUB - 1:
                edges[p, p + 1] = sub_bcast(cols[p + 1], p)
                pivot = sub_bcast(cols[p + 1], p + 1) - (sub_bcast(cols[p], p + 1) * inv) * edges[p, p + 1]
            invs.append(inv)
            scale = jnp.where(sub == p, inv, scale)
            top = sub_bcast(own, p)
            tops.append(top)
            if p < SUB - 1:
                mult = jnp.where(sub > p, cols[p] * inv, 0.0)
                for q in range(p + 1, SUB):
                    if q > p + 1:
                        edges[p, q] = sub_bcast(cols[q], p)
                    cols[q] = cols[q] - mult * edges[p, q]
                own = own - mult * top
        rows[k] = own
        scales.append(scale)
        for i in range(k + 1, count):
            below = [lane_bcast(rows[i], base + p) for p in range(SUB)]
            new = jnp.where(here, 0.0, rows[i])
            for p in range(SUB):
                mult = below[p] * invs[p]
                for q in range(p + 1, SUB):
                    below[q] = below[q] - mult * edges[p, q]
                new = new - mult * tops[p]
            rows[i] = new
        hook()
    return rows, scales

def exact(x, y, dims=NN):
    return lax.dot_general(x, y, dims, precision=HI, preferred_element_type=F32)


def factor_inverse(a, w, hook):
    n = a.shape[0]
    tiles = n // WIDE
    lane = lax.broadcasted_iota(jnp.int32, (WIDE, WIDE), 1)
    sub = lax.broadcasted_iota(jnp.int32, (WIDE, WIDE), 0)
    w[...] = jnp.zeros_like(w)
    waiting = []

    def between():
        if waiting:
            waiting.pop(0)()
        hook()

    def less(rows, cols, x, y):
        a[rows, cols] = a[rows, cols] - exact(x, y)

    for j in range(tiles):
        own = slice(j * WIDE, (j + 1) * WIDE)
        rows = [a[j * WIDE + SUB * k:j * WIDE + SUB * (k + 1), own] for k in range(WIDE // SUB)]
        rows, scales = factor_tile(rows, between)
        assert not waiting
        linv = jnp.where(lane <= sub, jnp.concatenate(rows, axis=0), 0.0)
        inv = jnp.concatenate(scales, axis=0)
        root = jnp.sqrt(inv)
        w[own, own] = linv * root
        if j + 1 == tiles:
            for i in range(j):
                at = slice(i * WIDE, (i + 1) * WIDE)
                w[own, at] = exact(linv, a[own, at]) * root
            break
        right, mult = {}, {}
        for i in range(j + 1, tiles):
            at = slice(i * WIDE, (i + 1) * WIDE)
            right[i] = a[own, at]
            mult[i] = a[at, own]

        def solve(i, linv=linv, inv=inv, right=right, mult=mult):
            right[i] = exact(linv, right[i]) * inv
            mult[i] = exact(mult[i], linv, NT)

        solve(j + 1)
        after = slice((j + 1) * WIDE, (j + 2) * WIDE)
        less(after, after, mult[j + 1], right[j + 1])

        for i in range(j + 2, tiles):
            waiting.append(functools.partial(solve, i))

        def update(i, j=j, own=own, linv=linv, inv=inv, right=right, mult=mult):
            at = slice(i * WIDE, (i + 1) * WIDE)
            for c in range(j + 1, tiles):
                if (i, c) != (j + 1, j + 1):
                    less(at, slice(c * WIDE, (c + 1) * WIDE), mult[i], right[c])
            a[at, own] = -exact(mult[i], linv * inv)

        def finish(c, j=j, own=own, linv=linv, inv=inv, root=root, mult=mult):
            at = slice(c * WIDE, (c + 1) * WIDE)
            left = exact(linv, a[own, at])
            w[own, at] = left * root
            left = left * inv
            for i in range(j + 1, tiles):
                less(slice(i * WIDE, (i + 1) * WIDE), at, mult[i], left)

        for i in range(j + 1, tiles):
            waiting.append(functools.partial(update, i))
        for c in range(j):
            waiting.append(functools.partial(finish, c))


class Net:
    def __init__(self, dims, send, recv):
        self.dims = dims
        me = lax.axis_index("wide")
        nx, nz, ny = dims
        self.me = (me // (nz * ny), (me // ny) % nz, me % ny)
        loop = lax.axis_index("loop")
        self.core = lax.rem(loop, 2)
        self.twin = {"loop": loop + 1 - 2 * self.core}
        self.send, self.recv, self.used, self.sent = send, recv, 0, []
        self.known = {}

    def peer(self, steps):
        c = [lax.rem(c + s, n) for c, s, n in zip(self.me, steps, self.dims)]
        return c, {"wide": (c[0] * self.dims[1] + c[1]) * self.dims[2] + c[2]}

    def along(self, axis, step):
        if (axis, step) not in self.known:
            c, device = self.peer([step if a == axis else 0 for a in range(3)])
            self.known[axis, step] = c[axis], device
        return self.known[axis, step]

    def plane(self):
        steps = [(0, dz, dy) for dz in range(self.dims[1]) for dy in range(self.dims[2]) if dz or dy]
        return sorted(steps, key=lambda s: -min(s[1], self.dims[1] - s[1]) - s[2])

    def slot(self):
        self.used += 1
        return self.used - 1

    def copy(self, src, dst, device, slot):
        pltpu.make_async_remote_copy(
            src_ref=src, dst_ref=dst, send_sem=self.send.at[slot], recv_sem=self.recv.at[slot], device_id=device, device_id_type=MESH
        ).start()

    def arrived(self, like, slot):
        pltpu.make_async_copy(like, like, self.recv.at[slot]).wait()
        self.sent.append((like, slot))

    def drain(self):
        for like, slot in self.sent:
            pltpu.make_async_copy(like, like, self.send.at[slot]).wait()

    def greet(self):
        devices = [self.peer(s)[1] for s in self.plane()] + [self.along(0, s)[1] for s in range(1, self.dims[0])] + [self.twin]
        for device in devices:
            pl.semaphore_signal(pltpu.get_barrier_semaphore(), inc=1, device_id=device, device_id_type=MESH)
        return len(devices)


class Reduced:
    def __init__(self, net, q, out, start, unit, order, bufs):
        self.net, self.q, self.out, self.start, self.order = net, q, out, start, order
        self.sizes = [net.dims[a] for a in order]
        self.coords = [net.me[a] for a in order]
        n1, n2, n3 = self.sizes
        self.blocks = [unit * n2 * n3, unit * n3, unit]
        self.bufs = bufs
        self.stage = 0

    def offset(self, level):
        at = self.start
        for l in range(level + 1):
            at = at + self.coords[l] * self.blocks[l]
        return pl.multiple_of(at, SUB)

    def source(self, level):
        return (self.q, self.start) if level == 0 else (self.bufs[level - 1][1], 0)

    def begin(self):
        self.slot = self.net.slot()
        level = min(self.stage, 5 - self.stage)
        size = self.blocks[level]
        for step in range(1, self.sizes[level]):
            at, device = self.net.along(self.order[level], step)
            if self.stage < 3:
                src, base = self.source(level)
                rows = pl.ds(pl.multiple_of(base + at * size, SUB), size)
                self.net.copy(src.at[rows], self.bufs[level][0].at[pl.ds((step - 1) * size, size)], device, self.slot)
            else:
                rows = pl.ds(self.offset(level), size)
                self.net.copy(self.out.at[rows], self.out.at[rows], device, self.slot)

    def finish(self):
        level = min(self.stage, 5 - self.stage)
        size, others = self.blocks[level], self.sizes[level] - 1
        if self.stage < 3:
            got, total = self.bufs[level]
            self.net.arrived(got, self.slot)
            src, base = self.source(level)
            acc = src[pl.ds(pl.multiple_of(base + self.coords[level] * size, SUB), size), :]
            for step in range(others):
                acc = acc + got[step * size:(step + 1) * size, :]
            if level < 2:
                total[...] = acc
            else:
                self.out[pl.ds(self.offset(2), size), :] = acc
        else:
            self.net.arrived(self.out.at[pl.ds(self.start, others * size)], self.slot)
        self.stage += 1

    def advance(self):
        self.finish()
        if self.stage < 6:
            self.begin()


class Diag:
    def __init__(self, net, g, like):
        self.net, self.g, self.like = net, g, like

    def spread(self):
        x, z, y = self.net.me
        own = self.g.at[self.net.core, x, z, y]
        self.slot = self.net.slot()
        for steps in self.net.plane():
            self.net.copy(own, own, self.net.peer(steps)[1], self.slot)

    def cross(self):
        nx, nz, ny = self.net.dims
        shape = self.g.shape
        self.net.arrived(self.like.at[pl.ds(0, (nz * ny - 1) * shape[4] * shape[5] // LANES)], self.slot)
        own = self.g.at[self.net.core, self.net.me[0]]
        self.slots = [self.net.slot() for _ in range(2 * nx)]
        for step in range(1, nx):
            self.net.copy(own, own, self.net.along(0, step)[1], self.slots[step])
        self.net.copy(own, own, self.net.twin, self.slots[nx])

    def swap(self):
        nx = self.net.dims[0]
        for step in range(1, nx):
            self.net.arrived(self.g.at[0, 0], self.slots[step])
            block = self.g.at[self.net.core, lax.rem(self.net.me[0] + nx - step, nx)]
            self.net.copy(block, block, self.net.twin, self.slots[nx + step])
        for step in range(nx):
            self.net.arrived(self.g.at[0, 0], self.slots[nx + step])


def scratch_for(dims, unit, orders):
    shapes = []
    for order in orders:
        n1, n2, n3 = [dims[a] for a in order]
        for level, (n, size) in enumerate(((n1, unit * n2 * n3), (n2, unit * n3), (n3, unit))):
            shapes += [pltpu.VMEM(((n - 1) * size, LANES), F32)] + [pltpu.VMEM((size, LANES), F32)] * (level < 2)
    return shapes


def split(x):
    hi = x.astype(BF16)
    return hi, (x - hi.astype(F32)).astype(BF16)

def dot3(a, b, dims):
    def one(x, y):
        return lax.dot_general(x, y, dims, preferred_element_type=F32)
    return one(a[0], b[0]) + (one(a[0], b[1]) + one(a[1], b[0]))

def select_rows(panel, tiles, q, tile):
    mine = panel.shape[0] // tile
    count, blocks = tiles.shape[0], panel.shape[1] // LANES
    first = lax.axis_index("wide") * mine
    wanted = [jnp.full((SUB, LANES), tiles[c] - first, jnp.int32) for c in range(count)]

    def step(r, carry):
        for cb in range(blocks):
            picked = [jnp.zeros((SUB, LANES), F32)] * count
            for i in range(mine):
                block = panel[pl.ds(pl.multiple_of(i * tile + r * SUB, SUB), SUB), cb * LANES:(cb + 1) * LANES]
                picked = [jnp.where(w == i, block, p) for w, p in zip(wanted, picked)]
            for c in range(count):
                q[pl.ds(pl.multiple_of((c * blocks + cb) * tile + r * SUB, SUB), SUB), :] = picked[c]
        return carry

    lax.fori_loop(0, tile // SUB, step, 0)


def front_kernel(dims, orders, groups, tile, d_ref, panel_hbm, t_in, tiles, mask, nh_ref, nl_ref, ph_ref, pl_ref, t_out, panel, q, g, a, w, out, local, send, recv, *bufs):
    n = a.shape[0]
    blocks = n // LANES
    half = n // 2
    net = Net(dims, send, recv)
    load = pltpu.make_async_copy(panel_hbm, panel, local.at[0])
    load.start()
    hand = pltpu.make_async_copy(t_in, t_out, local.at[1])
    hand.start()
    greeted = net.greet()
    g[net.core, net.me[0], net.me[1], net.me[2]] = d_ref[:, pl.ds(pl.multiple_of(net.core * half, LANES), half)]
    load.wait()
    select_rows(panel, tiles, q, tile)
    pl.semaphore_wait(pltpu.get_barrier_semaphore(), greeted)

    diag = Diag(net, g, q)
    diag.spread()
    rows = tile * blocks
    unit = rows // math.prod(dims)
    reduced = []
    for c, order in enumerate(orders):
        b = bufs[5 * c:5 * c + 5]
        reduced.append(Reduced(net, q, out, c * rows, unit, order, [(b[0], b[1]), (b[2], b[3]), (b[4], None)]))
        reduced[c].begin()
    for c in BEFORE:
        if c < 0:
            diag.cross()
        else:
            reduced[c].advance()

    def parts(r, carry):
        rows = pl.ds(pl.multiple_of(r * tile, tile), tile)
        ph_ref[rows, :], pl_ref[rows, :] = split(panel[rows, :])
        return carry

    lax.fori_loop(0, panel.shape[0] // tile, parts, 0)
    diag.swap()
    for h in range(2):
        a[:, h * half:(h + 1) * half] = g[h].reshape(n, half)

    later = list(LATER)
    calls = [0]

    def hook():
        while later and later[0][0] <= calls[0]:
            reduced[later.pop(0)[1]].advance()
        calls[0] += 1

    factor_inverse(a, w, hook)
    wt = split(w[...].T)
    inverse = split(dot3(wt, split(w[...]), NN))

    def emit(group):
        picked = [jnp.concatenate([out[c * rows + cb * tile:c * rows + (cb + 1) * tile, :] for cb in range(blocks)], axis=1) for c in group]
        hi, lo = split(dot3(split(jnp.concatenate(picked, axis=0)), inverse, NN))
        for i, c in enumerate(group):
            nh_ref[c * tile:(c + 1) * tile, :] = hi[i * tile:(i + 1) * tile]
            nl_ref[c * tile:(c + 1) * tile, :] = lo[i * tile:(i + 1) * tile]

    for k, group in enumerate(groups):
        for c in group:
            reduced[c].advance()
        group = sorted(group)
        emit(group)
        if k == 0:
            hand.wait()
        if k < len(groups) - 1:
            update_columns(tile, mask, group[0], len(group), ph_ref, pl_ref, nh_ref, nl_ref, t_out, t_out, lambda r: None)
    net.drain()


def front_call(dims, orders, groups, tile, diag, panel, trailing, tiles, mask):
    n, cols = panel.shape[1], tiles.shape[0] * tile
    total = cols * (n // LANES)
    unit = tile * (n // LANES) // math.prod(dims)
    sems = 1 + 2 * dims[0] + 6 * len(orders)
    V = pl.BlockSpec(memory_space=pltpu.VMEM)
    H = pl.BlockSpec(memory_space=pltpu.HBM)
    return pl.pallas_call(
        functools.partial(front_kernel, dims, orders, groups, tile),
        out_shape=(jax.ShapeDtypeStruct((cols, n), BF16),) * 2 + (jax.ShapeDtypeStruct(panel.shape, BF16),) * 2 + (jax.ShapeDtypeStruct(trailing.shape, F32),),
        in_specs=[V, H, H] + [pl.BlockSpec(memory_space=pltpu.SMEM)] * 2,
        out_specs=(V,) * 5,
        scratch_shapes=[
            pltpu.VMEM(panel.shape, F32), pltpu.VMEM((total, LANES), F32), pltpu.VMEM((2,) + dims + (diag.shape[0], n // 2), F32),
            pltpu.VMEM((n, n), F32), pltpu.VMEM((n, n), F32), pltpu.VMEM((total, LANES), F32), pltpu.SemaphoreType.DMA((2,)),
            pltpu.SemaphoreType.DMA((sems,)), pltpu.SemaphoreType.DMA((sems,)),
        ] + scratch_for(dims, unit, orders),
        cost_estimate=pl.CostEstimate(flops=10 * n**3, bytes_accessed=200_000_000, transcendentals=0),
        compiler_params=pltpu.CompilerParams(collective_id=0, has_side_effects=True, vmem_limit_bytes=FRONT_VMEM),
    )(diag, panel, trailing, tiles, mask)


def update_columns(tile, mask, first, count, ph_ref, pl_ref, nh_ref, nl_ref, t_ref, o_ref, after):
    rows = 4 * tile
    cols = slice(first * tile, (first + count) * tile)

    def step(r, carry):
        part = pl.ds(pl.multiple_of(r * rows, rows), rows)
        u = dot3((ph_ref[part, :], pl_ref[part, :]), (nh_ref[cols, :], nl_ref[cols, :]), NT)
        for i in range(rows // tile):
            at = pl.ds(pl.multiple_of(r * rows + i * tile, tile), tile)
            for j in range(count):
                c = slice((first + j) * tile, (first + j + 1) * tile)
                filled = jnp.full((tile, tile), mask[first + j, r * (rows // tile) + i], jnp.int32) != 0
                o_ref[at, c] = t_ref[at, c] - jnp.where(filled, u[i * tile:(i + 1) * tile, j * tile:(j + 1) * tile], 0.0)
        after(r)
        return carry

    lax.fori_loop(0, t_ref.shape[0] // rows, step, 0)


def update_kernel(tile, first, mask, ph_ref, pl_ref, t_ref, nh_ref, nl_ref, o_hbm, o, sems):
    steps = t_ref.shape[0] // (4 * tile)
    edge = first * tile

    def write(r, ref, cols, k):
        rows = pl.ds(pl.multiple_of(r * 4 * tile, 4 * tile), 4 * tile)
        return pltpu.make_async_copy(ref.at[rows, cols], o_hbm.at[rows, cols], sems.at[k, r])

    done, rest = slice(0, edge), slice(edge, t_ref.shape[1])
    for r in range(steps):
        write(r, t_ref, done, 0).start()
    update_columns(tile, mask, first, mask.shape[0] - first, ph_ref, pl_ref, nh_ref, nl_ref, t_ref, o, lambda r: write(r, o, rest, 1).start())
    for r in range(steps):
        write(r, t_ref, done, 0).wait()
        write(r, o, rest, 1).wait()


def update_call(ph, pl_, trailing, mask, nh, nl, tile, first):
    V = pl.BlockSpec(memory_space=pltpu.VMEM)
    return pl.pallas_call(
        functools.partial(update_kernel, tile, first),
        out_shape=jax.ShapeDtypeStruct(trailing.shape, F32),
        in_specs=[pl.BlockSpec(memory_space=pltpu.SMEM), V, V, V, V, V],
        out_specs=pl.BlockSpec(memory_space=pl.ANY),
        scratch_shapes=[pltpu.VMEM(trailing.shape, F32), pltpu.SemaphoreType.DMA((2, trailing.shape[0] // (4 * tile)))],
        compiler_params=pltpu.CompilerParams(vmem_limit_bytes=UPDATE_VMEM),
    )(mask, ph, pl_, trailing, nh, nl)


def shards(diag_block, panel, trailing, fill_mask, column_tiles):
    tile = trailing.shape[1] // column_tiles.shape[0]
    far = [pltpu.with_memory_space_constraint(x, pltpu.HBM) for x in (diag_block, panel, trailing, column_tiles, fill_mask.T)]
    high, low, panel_high, panel_low, kept = front_call(DIMS, ORDERS, GROUPS, tile, *far)
    return update_call(panel_high, panel_low, kept, far[4], high, low, tile, min(GROUPS[-1]))


def solution(mesh):
    return jax.shard_map(
        shards,
        mesh=mesh,
        in_specs=(P("wide", None), P("wide", None), P("wide", "loop"), P("wide", "loop"), P("loop")),
        out_specs=P("wide", "loop"),
        check_vma=False,
    )
```
